32 devices in a mesh: groups: 2 (over x), fsdp: 8 (over z, y), tensor: 2 (over core).
Axes of the slice: x: 2, y: 2, z: 4, core: 2. Of those that a mesh axis runs over, the one named last changes fastest.
Arguments:
- tokens: bfloat16 [16, 256, 8192], P(('groups', 'fsdp'), 'tensor'), parts along dimension 0, may hold values from -6 to 6
- norm_gain: float32 [8192], replicated, may hold values from 0.1 to 1.9
- blocks: bfloat16 [2, 768, 128, 128], P('tensor', 'fsdp'), may hold values from -0.09375 to 0.09375
- block_cols: int32 [2, 768], P('tensor', 'fsdp'), may hold values from -1 to 19, as said below
- key_cache: bfloat16 [16, 2048, 512], P(('groups', 'fsdp'), None, 'tensor'), parts along dimension 0, may hold values from -256 to 256
- value_cache: bfloat16 [16, 2048, 512], P(('groups', 'fsdp'), None, 'tensor'), parts along dimension 0, may hold values from -6 to 6
Outputs:
- attended: bfloat16 [16, 256, 4096], P(('groups', 'fsdp'), 'tensor'), parts along dimension 0
The draws below stay inside these ranges and needn't reach their ends.
There are 2 independent parts, one for each index of `groups`. The reference program is written for one: setup_inputs(seed, part) draws one part's arguments, and reference() takes and returns one part's arrays. A program takes and returns all parts, laid end to end along the dimension named above; an argument that names none is the same for every part. Nothing has to cross between parts.
Inputs may be any that keep to these rules, and one draw needn't show every extreme that they name: `block_cols`: the 12 slots s of row block r (s // 12 == r) of a head shard name distinct column blocks; between 8 and 12 of them are filled, the others are -1, and in every draw some row block of some shard fills all 12.
All inputs are finite; a program needn't handle non-finite values.
Results may differ from the reference program's by a relative error of at most 0.006.
The reference program's roundings to bfloat16 on the way (of `normed`, `queries` and `weights`) count: a program that leaves them out, or rounds other values in their place, can miss the bound.
Values may be sent and summed in bfloat16 or wider, within the bound.
A program may use at most 192 MiB of HBM per device.

```python
import math
import jax
import jax.numpy as jnp
from jax import lax

D = 8192
Q_HEADS = 32
KV_HEADS = 4
HEAD_DIM = 128
BLK = 128
RCAP = 12
SPAN = 256
PAST = 2048
SEQS = 8
NCOL = 20
SLOTS = 768
N_TENSOR = 2


def draw_block_cols(key, part):
    key = jax.random.fold_in(key, 11)
    first_key, second_key, third_key, fourth_key = jax.random.split(key, 4)
    row_total = N_TENSOR * (D // BLK)
    counts = jax.random.randint(first_key, (row_total,), NCOL - RCAP, RCAP + 1)
    fullest = jax.random.randint(second_key, (), 0, row_total)
    counts = jnp.where(jnp.arange(row_total) == fullest, RCAP, counts)
    chosen = jax.vmap(lambda single: jax.random.permutation(single, NCOL))(jax.random.split(third_key, row_total))[:, :RCAP]
    placing = jax.vmap(lambda single: jax.random.permutation(single, RCAP))(jax.random.split(fourth_key, row_total))
    columns = jnp.where(placing < counts[:, None], chosen, -1)
    return columns.reshape(N_TENSOR, D // BLK * RCAP).astype(jnp.int32)


def draw_key_cache(key, part):
    key = jax.random.fold_in(key, 23)
    normal_key = jax.random.fold_in(key, 0)
    base = jnp.clip(jax.random.normal(normal_key, (SEQS, PAST, KV_HEADS * HEAD_DIM), jnp.float32), -6.0, 6.0)
    return base.astype(jnp.bfloat16)


def levels(own_key, shape, cuts, low, top_value):
    level = 1.0
    for dim, shards_of in cuts:
        steps = jax.random.uniform(jax.random.fold_in(jax.random.fold_in(own_key, 6), dim), (shards_of,), jnp.float32, low / len(cuts), top_value / len(cuts))
        level = level * jnp.repeat(jnp.exp(steps), shape[dim] // shards_of).reshape((-1,) + (1,) * (len(shape) - 1 - dim))
    return level


def scatter_about(own_key, shape, spread, bound, cuts=(), kind=jnp.bfloat16):
    values = jax.random.normal(own_key, shape, jnp.float32) * spread
    if len(cuts) > 0:
        values = levels(own_key, shape, cuts, -0.22, 0.18) * values
    return jnp.clip(values, min=-bound, max=bound).astype(kind)


def setup_inputs(seed: int = 0, part: int = 0) -> dict:
    arg_keys = jax.random.split(jax.random.key(seed), 7)
    part_keys = jax.random.split(jax.random.fold_in(arg_keys[6], part), 7)
    tokens = scatter_about(part_keys[0], (SEQS, SPAN, D), 1.0, 6.0, ((0, 8), (1, 2)))
    norm_gain = jnp.clip(1.0 + 0.18 * jax.random.normal(arg_keys[1], (D,), jnp.float32), 0.1, 1.9)
    blocks = scatter_about(arg_keys[2], (N_TENSOR, SLOTS, BLK, BLK), (D // 2) ** -0.5, 0.09375, ((0, 2), (1, 8)))
    block_cols = draw_block_cols(jax.random.fold_in(arg_keys[6], 71), part)
    key_cache = draw_key_cache(jax.random.fold_in(jax.random.fold_in(arg_keys[6], part), 71), part)
    value_cache = scatter_about(part_keys[5], (SEQS, PAST, KV_HEADS * HEAD_DIM), 1.0, 6.0, ((0, 8), (2, 2)))
    return dict(tokens=tokens, norm_gain=norm_gain, blocks=blocks, block_cols=block_cols, key_cache=key_cache, value_cache=value_cache)


def rms_rows(values, norm_gain):
    widened = values.astype(jnp.float32)
    variance = lax.optimization_barrier(jnp.mean(widened * widened, axis=-1, keepdims=True))
    return (widened * lax.rsqrt(variance + 1e-05) * norm_gain).astype(jnp.bfloat16)

def rotate(values, offset):
    count = values.shape[-3]
    half_dim = values.shape[-1] // 2
    ladder = jnp.arange(half_dim, dtype=jnp.float32)
    inverse = 10000.0 ** (-2.0 * ladder / values.shape[-1])
    position = jnp.arange(count, dtype=jnp.float32) + offset
    angles = position[:, None] * inverse[None, :]
    cosine = jnp.cos(angles)[:, None, :]
    sine = jnp.sin(angles)[:, None, :]
    first_half = values[..., :half_dim]
    second_half = values[..., half_dim:]
    return jnp.concatenate([first_half * cosine - second_half * sine, second_half * cosine + first_half * sine], axis=-1)

def attend_group(queries, key_rows, value_rows, offset):
    span_rows = queries.shape[0]
    scale = 1.0 / math.sqrt(queries.shape[-1])
    scores = jnp.einsum('qgd,kd->gqk', queries.astype(jnp.float32), key_rows.astype(jnp.float32)) * scale
    query_pos = offset + jnp.arange(span_rows, dtype=jnp.int32)
    key_pos = jnp.arange(key_rows.shape[0], dtype=jnp.int32)
    allowed = key_pos[None, :] <= query_pos[:, None]
    scores = jnp.where(allowed[None], scores, -1e+30)
    highest = lax.optimization_barrier(jnp.max(scores, axis=-1, keepdims=True))
    expo = jnp.exp(scores - highest)
    denom = lax.optimization_barrier(jnp.sum(expo, axis=-1, keepdims=True))
    weights = lax.optimization_barrier(expo.astype(jnp.bfloat16))
    mixed = jnp.einsum('gqk,kd->qgd', weights.astype(jnp.float32), value_rows.astype(jnp.float32))
    mixed = mixed / jnp.transpose(denom, (1, 0, 2))
    return mixed.astype(jnp.bfloat16).reshape(span_rows, -1)

def project(flat_rows, shard_blocks, shard_cols):
    row_count = flat_rows.shape[1]
    weights = shard_blocks.reshape(row_count, RCAP, BLK, BLK)
    columns = shard_cols.reshape(row_count, RCAP)
    ladder = jnp.arange(NCOL, dtype=jnp.int32)

    def advance(running, inputs):
        row_values, row_weights, row_columns = inputs
        products = jnp.einsum('tk,skj->tsj', row_values.astype(jnp.float32), row_weights.astype(jnp.float32), precision=lax.Precision.HIGHEST)
        selector = (row_columns[:, None] == ladder[None, :]).astype(jnp.float32)
        return (running + jnp.einsum('tsj,sc->tcj', products, selector, precision=lax.Precision.HIGHEST), None)
    initial = jnp.zeros((flat_rows.shape[0], NCOL, BLK), jnp.float32)
    result, ignored = lax.scan(advance, initial, (jnp.swapaxes(flat_rows, 0, 1), weights, columns))
    return result

def reference(tokens, norm_gain, blocks, block_cols, key_cache, value_cache):
    normed = lax.optimization_barrier(rms_rows(tokens, norm_gain))
    flat_rows = normed.reshape(SEQS * SPAN, D // BLK, BLK)
    local_heads = Q_HEADS // N_TENSOR
    key_heads = KV_HEADS // N_TENSOR
    group_size = Q_HEADS // KV_HEADS
    query_cols = local_heads * HEAD_DIM
    key_cols = key_heads * HEAD_DIM
    pieces = []
    for shard in range(N_TENSOR):
        projected = project(flat_rows, blocks[shard], block_cols[shard]).reshape(SEQS, SPAN, NCOL * BLK)
        queries = rotate(projected[..., :query_cols].reshape(SEQS, SPAN, local_heads, HEAD_DIM), PAST).astype(jnp.bfloat16)
        new_keys = rotate(projected[..., query_cols:query_cols + key_cols].reshape(SEQS, SPAN, key_heads, HEAD_DIM), PAST).astype(jnp.bfloat16)
        new_values = projected[..., query_cols + key_cols:].astype(jnp.bfloat16).reshape(SEQS, SPAN, key_heads, HEAD_DIM)
        queries = lax.optimization_barrier(queries)
        new_keys = lax.optimization_barrier(new_keys)
        new_values = lax.optimization_barrier(new_values)
        cached_keys = key_cache[:, :, shard * key_cols:(shard + 1) * key_cols].reshape(SEQS, PAST, key_heads, HEAD_DIM)
        cached_values = value_cache[:, :, shard * key_cols:(shard + 1) * key_cols].reshape(SEQS, PAST, key_heads, HEAD_DIM)
        all_keys = jnp.concatenate([cached_keys, new_keys], axis=1)
        all_values = jnp.concatenate([cached_values, new_values], axis=1)

        def one_sequence(inputs):
            query_seq, key_seq, value_seq = inputs
            mixed = [attend_group(query_seq[:, group_index * group_size:(group_index + 1) * group_size], key_seq[:, group_index], value_seq[:, group_index], PAST) for group_index in range(key_heads)]
            return jnp.concatenate(mixed, axis=-1)
        pieces.append(lax.map(one_sequence, (queries, all_keys, all_values)))
    return jnp.concatenate(pieces, axis=-1)
```

```python
import functools
import math

import jax
import jax.numpy as jnp
import numpy as np
from jax import lax
from jax.experimental import pallas as pl
from jax.experimental.pallas import tpu as pltpu
from jax.sharding import PartitionSpec as P

D = 8192
Q_HEADS = 32
KV_HEADS = 4
HEAD_DIM = 128
BLK = 128
RCAP = 12
MESH = pl.DeviceIdType.MESH
SUB = 2


def rms_rows(values, norm_gain):
    widened = values.astype(jnp.float32)
    variance = jnp.mean(widened * widened, axis=-1, keepdims=True)
    return (widened * lax.rsqrt(variance + 1e-05) * norm_gain).astype(jnp.bfloat16)


def ring_shape(count):
    fast = 2 ** (int(math.log2(count)) // 2)
    return count // fast, fast


def ring_position(index, count):
    rows, fast = ring_shape(count)
    row, col = index // fast, index % fast
    turned = jnp.where(row % 2 == 0, col - 1, fast - 1 - col)
    inside = 1 + row * (fast - 1) + turned
    back = lax.rem(count - row, count)
    return jnp.where(col == 0, back, inside)


def ring_index(position, count):
    rows, fast = ring_shape(count)
    pos = jnp.where(position == 0, count, position)
    row_in = (pos - 1) // (fast - 1)
    k = (pos - 1) % (fast - 1)
    col_in = jnp.where(row_in % 2 == 0, 1 + k, fast - 1 - k)
    inside = row_in * fast + col_in
    back = (count - pos) * fast
    return jnp.where(pos <= rows * (fast - 1), inside, back)


def gather_kernel(count, normed, blocks, tokens_out, weights,
                  ring_send, ring_recv, sib_send, sib_recv, own_send, own_recv,
                  tok_send, tok_recv, local_sem):
    x = lax.axis_index("groups")
    f = lax.axis_index("fsdp")
    c = lax.axis_index("tensor")
    position = ring_position(f, count)
    step = 1 - 2 * c
    ahead = ring_index(lax.rem(position + step + count, count), count)
    behind = ring_index(lax.rem(position - step + count, count), count)

    barrier = pltpu.get_barrier_semaphore()
    for peer in ((x, f, 1 - c), (1 - x, f, c), (1 - x, f, 1 - c), (x, ahead, c), (x, behind, c)):
        pl.semaphore_signal(barrier, inc=1, device_id=peer, device_id_type=MESH)
    pl.semaphore_wait(barrier, 5)

    def own(half, k, src):
        return pltpu.make_async_remote_copy(
            src_ref=src, dst_ref=weights.at[f, half, k],
            send_sem=own_send.at[half, k], recv_sem=own_recv.at[half, k],
            device_id=(x, f, 1 - c), device_id_type=MESH)

    def own_local(half, k):
        return pltpu.make_async_copy(blocks.at[half, k], weights.at[f, half, k], local_sem.at[half, k])

    def ring(s, k):
        origin = ring_index(lax.rem(position - (s - 1) * step + count * 2, count), count)
        return pltpu.make_async_remote_copy(
            src_ref=weights.at[origin, c, k], dst_ref=weights.at[origin, c, k],
            send_sem=ring_send.at[s - 1, k], recv_sem=ring_recv.at[s - 1, k],
            device_id=(x, ahead, c), device_id_type=MESH)

    def sibling(s, k):
        origin = ring_index(lax.rem(position - s * step + count * 2, count), count)
        return pltpu.make_async_remote_copy(
            src_ref=weights.at[origin, c, k], dst_ref=weights.at[origin, c, k],
            send_sem=sib_send.at[s - 1, k], recv_sem=sib_recv.at[s - 1, k],
            device_id=(x, f, 1 - c), device_id_type=MESH)

    def arrived(s, k):
        origin = ring_index(lax.rem(position - s * step + count * 2, count), count)
        return pltpu.make_async_remote_copy(
            src_ref=weights.at[origin, c, k], dst_ref=weights.at[origin, c, k],
            send_sem=ring_send.at[s - 1, k], recv_sem=ring_recv.at[s - 1, k],
            device_id=(x, ahead, c), device_id_type=MESH)

    def sibling_arrived(s, k):
        origin = ring_index(lax.rem(position + s * step + count * 2, count), count)
        return pltpu.make_async_remote_copy(
            src_ref=weights.at[origin, 1 - c, k], dst_ref=weights.at[origin, 1 - c, k],
            send_sem=sib_send.at[s - 1, k], recv_sem=sib_recv.at[s - 1, k],
            device_id=(x, f, 1 - c), device_id_type=MESH)

    def token(plane):
        return pltpu.make_async_remote_copy(
            src_ref=normed, dst_ref=tokens_out.at[c],
            send_sem=tok_send.at[plane], recv_sem=tok_recv.at[c],
            device_id=(plane, f, x), device_id_type=MESH)

    def token_arrived(half):
        return pltpu.make_async_remote_copy(
            src_ref=normed, dst_ref=tokens_out.at[half],
            send_sem=tok_send.at[0], recv_sem=tok_recv.at[half],
            device_id=(1 - x, f, x), device_id_type=MESH)

    def token_local():
        return pltpu.make_async_copy(normed, tokens_out.at[c], local_sem.at[2, 0])

    owner = x == c

    @pl.when(owner)
    def _():
        for k in range(SUB):
            own_local(c, k).start()
            own(1 - c, k, blocks.at[1 - c, k]).start()
        for k in range(SUB):
            own_local(c, k).wait()
            ring(1, k).start()
        for k in range(SUB):
            own_local(1 - c, k).start()
            own(c, k, blocks.at[c, k]).start()
        token(1 - x).start()
        token_local().start()

    @pl.when(jnp.logical_not(owner))
    def _():
        for k in range(SUB):
            own(c, k, blocks.at[c, k]).wait_recv()
            ring(1, k).start()
        token(1 - x).start()
        token(x).start()

    def advance(s, carry):
        for k in range(SUB):
            arrived(s, k).wait_recv()

            @pl.when(s < count - 1)
            def _():
                ring(s + 1, k).start()

            sibling(s, k).start()
        return carry

    lax.fori_loop(1, count, advance, 0)

    def finish(s, carry):
        for k in range(SUB):
            ring(s, k).wait_send()
            sibling(s, k).wait_send()
            sibling_arrived(s, k).wait_recv()
        return carry

    lax.fori_loop(1, count, finish, 0)

    @pl.when(owner)
    def _():
        for k in range(SUB):
            own(1 - c, k, blocks.at[1 - c, k]).wait_send()
            own(c, k, blocks.at[c, k]).wait_send()
            own_local(1 - c, k).wait()
        token(1 - x).wait_send()
        token_local().wait()
        token_arrived(1 - c).wait_recv()

    @pl.when(jnp.logical_not(owner))
    def _():
        for k in range(SUB):
            own(1 - c, k, blocks.at[1 - c, k]).wait_recv()
        token(1 - x).wait_send()
        token(x).wait_send()
        token_arrived(0).wait_recv()
        token_arrived(1).wait_recv()


def gather(count, normed, blocks):
    slots = blocks.shape[0]
    piece = slots // (2 * SUB)
    half_rows, width = normed.shape
    any_space = pl.BlockSpec(memory_space=pl.ANY)
    dma = pltpu.SemaphoreType.DMA
    return pl.pallas_call(
        functools.partial(gather_kernel, count),
        out_shape=(
            jax.ShapeDtypeStruct((2, half_rows, width), jnp.bfloat16),
            jax.ShapeDtypeStruct((count, 2, SUB, piece, BLK, BLK), jnp.bfloat16),
        ),
        in_specs=[any_space] * 2,
        out_specs=(any_space, any_space),
        scratch_shapes=[
            dma((count - 1, SUB)), dma((count - 1, SUB)),
            dma((count - 1, SUB)), dma((count - 1, SUB)),
            dma((2, SUB)), dma((2, SUB)),
            dma((2,)), dma((2,)), dma((3, SUB)),
        ],
        compiler_params=pltpu.CompilerParams(collective_id=0, has_side_effects=True),
    )(normed, blocks.reshape(2, SUB, piece, BLK, BLK))


def project_kernel(group, ncol, rot_heads, cols, x_ref, w_ref, cos_ref, sin_ref, out_ref, panel, acc):
    i = pl.program_id(0)

    def place(r, carry):
        rows = pl.ds(pl.multiple_of(r * BLK, BLK), BLK)
        panel[rows, :] = jnp.zeros((BLK, panel.shape[1]), jnp.bfloat16)
        for s in range(RCAP):
            col = cols[(i * group + r) * RCAP + s]
            col = jnp.where(col < 0, ncol, col)
            panel[rows, pl.ds(pl.multiple_of(col * BLK, BLK), BLK)] = w_ref[r * RCAP + s]
        return carry

    lax.fori_loop(0, group, place, 0)

    @pl.when(i == 0)
    def _():
        acc[...] = jnp.zeros_like(acc)

    step = 4 * BLK
    for j in range(0, ncol * BLK, step):
        acc[:, j:j + step] += jnp.dot(
            x_ref[...], panel[:, j:j + step], preferred_element_type=jnp.float32)

    @pl.when(i == pl.num_programs(0) - 1)
    def _():
        for h in range(ncol):
            part = acc[:, h * BLK:(h + 1) * BLK]
            if h < rot_heads:
                part = part * cos_ref[...] + pltpu.roll(part, BLK // 2, 1) * sin_ref[...]
            out_ref[:, h * BLK:(h + 1) * BLK] = part.astype(jnp.bfloat16)


def project(normed, weights, cols, cosine, sine, ncol, rot_heads):
    span, width = normed.shape
    group = 8
    grid = width // BLK // group
    return pl.pallas_call(
        functools.partial(project_kernel, group, ncol, rot_heads),
        out_shape=jax.ShapeDtypeStruct((span, ncol * BLK), jnp.bfloat16),
        grid_spec=pltpu.PrefetchScalarGridSpec(
            num_scalar_prefetch=1,
            grid=(grid,),
            in_specs=[
                pl.BlockSpec((span, group * BLK), lambda i, c: (0, i)),
                pl.BlockSpec((group * RCAP, BLK, BLK), lambda i, c: (i, 0, 0)),
                pl.BlockSpec((span, HEAD_DIM), lambda i, c: (0, 0)),
                pl.BlockSpec((span, HEAD_DIM), lambda i, c: (0, 0)),
            ],
            out_specs=pl.BlockSpec((span, ncol * BLK), lambda i, c: (0, 0)),
            scratch_shapes=[
                pltpu.VMEM((group * BLK, (ncol + 1) * BLK), jnp.bfloat16),
                pltpu.VMEM((span, ncol * BLK), jnp.float32),
            ],
        ),
        compiler_params=pltpu.CompilerParams(vmem_limit_bytes=48 * 2**20),
    )(cols, normed, weights, cosine, sine)


def attend_kernel(q_ref, kn_ref, vn_ref, kc_ref, vc_ref, out_ref):
    dims = (((1,), (1,)), ((), ()))
    factor = math.log2(math.e) / math.sqrt(HEAD_DIM)
    q = q_ref[...]
    old = lax.dot_general(q, kc_ref[...], dims, preferred_element_type=jnp.float32)
    new = lax.dot_general(q, kn_ref[...], dims, preferred_element_type=jnp.float32)
    row = lax.broadcasted_iota(jnp.int32, new.shape, 0)
    col = lax.broadcasted_iota(jnp.int32, new.shape, 1)
    new = jnp.where(col <= row, new, -1e30)
    highest = jnp.maximum(
        jnp.max(old, axis=-1, keepdims=True), jnp.max(new, axis=-1, keepdims=True))
    old = jnp.exp2((old - highest) * factor)
    new = jnp.exp2((new - highest) * factor)
    denom = jnp.sum(old, axis=-1, keepdims=True) + jnp.sum(new, axis=-1, keepdims=True)
    mixed = jnp.dot(old.astype(jnp.bfloat16), vc_ref[...], preferred_element_type=jnp.float32)
    mixed += jnp.dot(new.astype(jnp.bfloat16), vn_ref[...], preferred_element_type=jnp.float32)
    out_ref[...] = (mixed / denom).astype(jnp.bfloat16)


def attend(qkv, keys, values, heads, key_heads):
    span = qkv.shape[0]
    past = keys.shape[0]
    share = heads // key_heads
    return pl.pallas_call(
        attend_kernel,
        out_shape=jax.ShapeDtypeStruct((span, heads * HEAD_DIM), jnp.bfloat16),
        grid=(heads,),
        in_specs=[
            pl.BlockSpec((span, HEAD_DIM), lambda h: (0, h)),
            pl.BlockSpec((span, HEAD_DIM), lambda h: (0, heads + h // share)),
            pl.BlockSpec((span, HEAD_DIM), lambda h: (0, heads + key_heads + h // share)),
            pl.BlockSpec((past, HEAD_DIM), lambda h: (0, h // share)),
            pl.BlockSpec((past, HEAD_DIM), lambda h: (0, h // share)),
        ],
        out_specs=pl.BlockSpec((span, HEAD_DIM), lambda h: (0, h)),
        compiler_params=pltpu.CompilerParams(vmem_limit_bytes=48 * 2**20),
    )(qkv, qkv, qkv, keys, values)


def rope_tables(span, offset):
    half = HEAD_DIM // 2
    inverse = np.float32(10000.0) ** (np.float32(-2.0) * np.arange(half, dtype=np.float32) / np.float32(HEAD_DIM))
    angles = (np.arange(span, dtype=np.float32) + np.float32(offset))[:, None] * inverse[None, :]
    angles = angles.astype(np.float64)
    cosine, sine = np.cos(angles), np.sin(angles)
    return (
        np.concatenate([cosine, cosine], axis=1).astype(np.float32),
        np.concatenate([-sine, sine], axis=1).astype(np.float32),
    )


def on_device(tokens, norm_gain, blocks, block_cols, key_cache, value_cache):
    tensor_count = lax.axis_size("tensor")
    count = lax.axis_size("fsdp")
    heads = Q_HEADS // tensor_count
    key_heads = KV_HEADS // tensor_count
    ncol = (heads + 2 * key_heads) * HEAD_DIM // BLK
    span = tokens.shape[1] * tensor_count
    every = lax.all_gather(block_cols[0], ("tensor", "fsdp"), axis=0, tiled=True)
    every = every.reshape(tensor_count, -1)
    cols = lax.dynamic_index_in_dim(every, lax.axis_index("groups"), 0, keepdims=False)
    normed, weights = gather(count, rms_rows(tokens[0], norm_gain), blocks[0])
    cosine, sine = rope_tables(span, key_cache.shape[1])
    qkv = project(
        normed.reshape(span, D), weights.reshape(-1, BLK, BLK), cols,
        jnp.asarray(cosine), jnp.asarray(sine), ncol, heads + key_heads)
    swaps = [(a * 2 + b, b * 2 + a) for a in range(2) for b in range(2)]
    qkv = lax.ppermute(qkv, ("groups", "tensor"), swaps)
    attended = attend(qkv, key_cache[0], value_cache[0], heads, key_heads)
    result = lax.all_to_all(attended, "tensor", split_axis=0, concat_axis=1, tiled=True)
    return result[None]


def solution(mesh):
    in_specs = (
        P(("groups", "fsdp"), "tensor", None),
        P(),
        P("tensor", "fsdp", None, None),
        P("tensor", "fsdp"),
        P(("groups", "fsdp"), None, "tensor"),
        P(("groups", "fsdp"), None, "tensor"),
    )
    out_specs = P(("groups", "fsdp"), "tensor", None)
    return jax.shard_map(
        on_device, mesh=mesh, in_specs=in_specs, out_specs=out_specs, check_vma=False
    )
```

```python
import functools
import math

import jax
import jax.numpy as jnp
import numpy as np
from jax import lax
from jax.experimental import pallas as pl
from jax.experimental.pallas import tpu as pltpu
from jax.sharding import PartitionSpec as P

D = 8192
Q_HEADS = 32
KV_HEADS = 4
HEAD_DIM = 128
BLK = 128
RCAP = 12
MESH = pl.DeviceIdType.MESH


def ring_shape(count):
    fast = 2 ** (int(math.log2(count)) // 2)
    return count // fast, fast


def ring_position(index, count):
    rows, fast = ring_shape(count)
    row, col = index // fast, index % fast
    turned = jnp.where(row % 2 == 0, col - 1, fast - 1 - col)
    inside = 1 + row * (fast - 1) + turned
    back = lax.rem(count - row, count)
    return jnp.where(col == 0, back, inside)


def ring_index(position, count):
    rows, fast = ring_shape(count)
    pos = jnp.where(position == 0, count, position)
    row_in = (pos - 1) // (fast - 1)
    k = (pos - 1) % (fast - 1)
    col_in = jnp.where(row_in % 2 == 0, 1 + k, fast - 1 - k)
    inside = row_in * fast + col_in
    back = (count - pos) * fast
    return jnp.where(pos <= rows * (fast - 1), inside, back)


def fused_kernel(count, ncol, rot_heads, tokens, gain, cos_ref, sin_ref, blocks, places,
                 qkv_out, weights, every_place,
                 mine, normed, stage_own, stage_sib, place_own, place_sib, panel, acc, ready,
                 ring_send, ring_recv, sib_send, sib_recv, own_send, own_recv,
                 tok_send, tok_recv, swap_send, swap_recv, local_sem, stage_sem):
    x = lax.axis_index("groups")
    f = lax.axis_index("fsdp")
    c = lax.axis_index("tensor")
    position = ring_position(f, count)
    step = 1 - 2 * c
    ahead = ring_index(lax.rem(position + step + count, count), count)
    behind = ring_index(lax.rem(position - step + count, count), count)
    slots = blocks.shape[1]
    sub = ring_send.shape[1] - 1
    piece = slots // sub
    half_rows = tokens.shape[0]
    width = tokens.shape[1]
    per_origin = width // count
    depth = panel.shape[0]
    owner = x == c
    guest = jnp.logical_not(owner)

    barrier = pltpu.get_barrier_semaphore()
    for peer in ((x, f, 1 - c), (1 - x, f, c), (1 - x, f, 1 - c), (x, ahead, c), (x, behind, c)):
        pl.semaphore_signal(barrier, inc=1, device_id=peer, device_id_type=MESH)
    pl.semaphore_wait(barrier, 5)

    def held(origin, half, k):
        if k == sub:
            return every_place.at[origin, half]
        return weights.at[origin, half, pl.ds(k * piece, piece)]

    def given(half, k):
        if k == sub:
            return places.at[half]
        return blocks.at[half, pl.ds(k * piece, piece)]

    def own(half, k):
        return pltpu.make_async_remote_copy(
            src_ref=given(half, k), dst_ref=held(f, half, k),
            send_sem=own_send.at[half, k], recv_sem=own_recv.at[half, k],
            device_id=(x, f, 1 - c), device_id_type=MESH)

    def own_local(half, k):
        return pltpu.make_async_copy(given(half, k), held(f, half, k), local_sem.at[half, k])

    def from_behind(s):
        return ring_index(lax.rem(position - s * step + count * 2, count), count)

    def from_sibling(s):
        return ring_index(lax.rem(position + s * step + count * 2, count), count)

    def ring(s, k):
        ref = held(from_behind(s - 1), c, k)
        return pltpu.make_async_remote_copy(
            src_ref=ref, dst_ref=ref,
            send_sem=ring_send.at[s - 1, k], recv_sem=ring_recv.at[s - 1, k],
            device_id=(x, ahead, c), device_id_type=MESH)

    def arrived(s, k):
        ref = held(from_behind(s), c, k)
        return pltpu.make_async_remote_copy(
            src_ref=ref, dst_ref=ref,
            send_sem=ring_send.at[s - 1, k], recv_sem=ring_recv.at[s - 1, k],
            device_id=(x, ahead, c), device_id_type=MESH)

    def sibling(s, k):
        ref = held(from_behind(s), c, k)
        return pltpu.make_async_remote_copy(
            src_ref=ref, dst_ref=ref,
            send_sem=sib_send.at[s - 1, k], recv_sem=sib_recv.at[s - 1, k],
            device_id=(x, f, 1 - c), device_id_type=MESH)

    def sibling_arrived(s, k):
        ref = held(from_sibling(s), 1 - c, k)
        return pltpu.make_async_remote_copy(
            src_ref=ref, dst_ref=ref,
            send_sem=sib_send.at[s - 1, k], recv_sem=sib_recv.at[s - 1, k],
            device_id=(x, f, 1 - c), device_id_type=MESH)

    def token_rows(half):
        return normed.at[pl.ds(pl.multiple_of(half * half_rows, half_rows), half_rows)]

    def token(plane):
        return pltpu.make_async_remote_copy(
            src_ref=mine, dst_ref=token_rows(c),
            send_sem=tok_send.at[plane], recv_sem=tok_recv.at[c],
            device_id=(plane, f, x), device_id_type=MESH)

    def token_arrived(half):
        return pltpu.make_async_remote_copy(
            src_ref=mine, dst_ref=token_rows(half),
            send_sem=tok_send.at[0], recv_sem=tok_recv.at[half],
            device_id=(1 - x, f, x), device_id_type=MESH)

    def token_local():
        return pltpu.make_async_copy(mine, token_rows(c), local_sem.at[2, 0])

    @pl.when(owner)
    def _():
        for k in range(sub + 1):
            own_local(c, k).start()
            own(1 - c, k).start()
        for k in range(sub + 1):
            own_local(c, k).wait()
        for k in range(sub + 1):
            own_local(1 - c, k).start()
            own(c, k).start()

    @pl.when(guest)
    def _():
        for k in range(sub + 1):
            own(c, k).wait_recv()

    ring(1, sub).start()
    ring(1, 0).start()
    ring(1, 1).start()

    def norm_rows(i, carry):
        rows = pl.ds(pl.multiple_of(i * 16, 16), 16)
        wide = tokens[rows, :].astype(jnp.float32)
        variance = jnp.mean(wide * wide, axis=-1, keepdims=True)
        mine[rows, :] = (wide * lax.rsqrt(variance + 1e-05) * gain[...]).astype(jnp.bfloat16)
        return carry

    lax.fori_loop(0, half_rows // 16, norm_rows, 0)
    token(1 - x).start()

    @pl.when(owner)
    def _():
        token_local().start()

    @pl.when(guest)
    def _():
        token(x).start()

    for k in range(2, sub):
        ring(1, k - 2).wait_send()
        ring(1, k).start()

    acc[...] = jnp.zeros_like(acc)
    for stage in (stage_own, stage_sib):
        stage[slots] = jnp.zeros((BLK, BLK), jnp.bfloat16)

    def pass_on(s, k):
        arrived(s, k).wait_recv()

        @pl.when(s < count - 1)
        def _():
            if k < sub:
                if k >= 2:
                    ring(s + 1, k - 2).wait_send()
                else:
                    ring(s, sub + k - 2).wait_send()
            ring(s + 1, k).start()

        sibling(s, k).start()

    order = [sub] + list(range(sub))

    def stage_copies(origin, half, stage, place, which):
        return (
            pltpu.make_async_copy(weights.at[origin, half], stage.at[pl.ds(0, slots)], stage_sem.at[which, 0]),
            pltpu.make_async_copy(every_place.at[origin, half], place, stage_sem.at[which, 1]),
        )

    def multiply(origin, half, stage, place):
        def fill(r, carry):
            rows = pl.ds(pl.multiple_of(r * BLK, BLK), BLK)
            for col in range(ncol):
                panel[rows, col * BLK:(col + 1) * BLK] = stage[place[r, col]]
            return carry

        lax.fori_loop(0, depth // BLK, fill, 0)
        start = origin * per_origin + half * (per_origin - depth)
        part = normed[:, pl.ds(pl.multiple_of(start, BLK), depth)]
        wide = 4 * BLK
        for j in range(0, ncol * BLK, wide):
            acc[:, j:j + wide] += jnp.dot(
                part, panel[:, j:j + wide], preferred_element_type=jnp.float32)

    def task(j, which):
        if which == 0:
            origin, half, stage, place = from_behind(j), c, stage_own, place_own
        else:
            origin, half, stage, place = from_sibling(j), 1 - c, stage_sib, place_sib

            @pl.when(j > 0)
            def _():
                for k in range(sub + 1):
                    sibling_arrived(j, k).wait_recv()
        copies = stage_copies(origin, half, stage, place, which)
        for copy in copies:
            copy.start()
        for copy in copies:
            copy.wait()
        multiply(origin, half, stage, place)

    def early(s, carry):
        for k in order:
            pass_on(s, k)
        return carry

    lax.fori_loop(1, count // 2, early, 0)

    @pl.when(owner)
    def _():
        for k in range(sub + 1):
            own_local(1 - c, k).wait()
        token_local().wait()
        token_arrived(1 - c).wait_recv()

    @pl.when(guest)
    def _():
        for k in range(sub + 1):
            own(1 - c, k).wait_recv()
        token_arrived(0).wait_recv()
        token_arrived(1).wait_recv()

    def late(s, carry):
        first = 2 * (s - count // 2)
        pass_on(s, sub)
        for k in range(sub):
            pass_on(s, k)
            for t in range(4):
                if min(t, sub - 1) != k:
                    continue
                if t < 2:
                    task(first, t)
                else:
                    @pl.when(first + 1 < count - 1)
                    def _():
                        task(first + 1, t - 2)
        return carry

    lax.fori_loop(count // 2, count, late, 0)
    task(count - 1, 0)
    task(count - 1, 1)

    part_width = 4 * BLK
    parts = ncol * BLK // part_width

    def swap(i):
        cols = pl.ds(i * part_width, part_width)
        return pltpu.make_async_remote_copy(
            src_ref=ready.at[:, cols], dst_ref=qkv_out.at[:, cols],
            send_sem=swap_send.at[i], recv_sem=swap_recv.at[i],
            device_id=(c, f, x), device_id_type=MESH)

    def keep(i):
        cols = pl.ds(i * part_width, part_width)
        return pltpu.make_async_copy(ready.at[:, cols], qkv_out.at[:, cols], swap_send.at[i])

    for i in range(parts):
        for h in range(i * part_width // BLK, (i + 1) * part_width // BLK):
            head = acc[:, h * BLK:(h + 1) * BLK]
            if h < rot_heads:
                head = head * cos_ref[...] + pltpu.roll(head, BLK // 2, 1) * sin_ref[...]
            ready[:, h * BLK:(h + 1) * BLK] = head.astype(jnp.bfloat16)

        @pl.when(owner)
        def _():
            keep(i).start()

        @pl.when(guest)
        def _():
            swap(i).start()

    ring(count - 1, sub - 2).wait_send()
    ring(count - 1, sub - 1).wait_send()

    def finish(s, carry):
        ring(s, sub).wait_send()
        for k in range(sub + 1):
            sibling(s, k).wait_send()
        return carry

    lax.fori_loop(1, count, finish, 0)
    token(1 - x).wait_send()

    @pl.when(owner)
    def _():
        for k in range(sub + 1):
            own(1 - c, k).wait_send()
            own(c, k).wait_send()
        for i in range(parts):
            keep(i).wait()

    @pl.when(guest)
    def _():
        token(x).wait_send()
        for i in range(parts):
            swap(i).wait_send()
            swap(i).wait_recv()


def project(count, tokens, norm_gain, blocks, places, cosine, sine, ncol, rot_heads):
    slots = blocks.shape[1]
    sub = max([option for option in (4, 3, 2) if slots % option == 0])
    half_rows, width = tokens.shape
    span = cosine.shape[0]
    depth = max(width // BLK // count // 2, 1) * BLK
    any_space = pl.BlockSpec(memory_space=pl.ANY)
    in_vmem = pl.BlockSpec(memory_space=pltpu.VMEM)
    dma = pltpu.SemaphoreType.DMA
    bf16 = jnp.bfloat16
    return pl.pallas_call(
        functools.partial(fused_kernel, count, ncol, rot_heads),
        out_shape=(
            jax.ShapeDtypeStruct((span, ncol * BLK), bf16),
            jax.ShapeDtypeStruct((count, 2, slots, BLK, BLK), bf16),
            jax.ShapeDtypeStruct((count,) + places.shape, jnp.int32),
        ),
        in_specs=[in_vmem] * 4 + [any_space] * 2,
        out_specs=(any_space,) * 3,
        scratch_shapes=[
            pltpu.VMEM((half_rows, width), bf16),
            pltpu.VMEM((span, width), bf16),
            pltpu.VMEM((slots + 1, BLK, BLK), bf16),
            pltpu.VMEM((slots + 1, BLK, BLK), bf16),
            pltpu.SMEM(places.shape[1:], jnp.int32),
            pltpu.SMEM(places.shape[1:], jnp.int32),
            pltpu.VMEM((depth, ncol * BLK), bf16),
            pltpu.VMEM((span, ncol * BLK), jnp.float32),
            pltpu.VMEM((span, ncol * BLK), bf16),
            dma((count - 1, sub + 1)), dma((count - 1, sub + 1)),
            dma((count - 1, sub + 1)), dma((count - 1, sub + 1)),
            dma((2, sub + 1)), dma((2, sub + 1)),
            dma((2,)), dma((2,)), dma((8,)), dma((8,)), dma((3, sub + 1)), dma((2, 2)),
        ],
        compiler_params=pltpu.CompilerParams(
            collective_id=0, has_side_effects=True, vmem_limit_bytes=56 * 2**20),
    )(tokens, norm_gain[None], cosine, sine, blocks, places)


def attend_kernel(q_ref, kn_ref, vn_ref, kc_ref, vc_ref, out_ref):
    dims = (((1,), (1,)), ((), ()))
    factor = math.log2(math.e) / math.sqrt(HEAD_DIM)
    q = q_ref[...]
    old = lax.dot_general(q, kc_ref[...], dims, preferred_element_type=jnp.float32)
    new = lax.dot_general(q, kn_ref[...], dims, preferred_element_type=jnp.float32)
    row = lax.broadcasted_iota(jnp.int32, new.shape, 0)
    col = lax.broadcasted_iota(jnp.int32, new.shape, 1)
    new = jnp.where(col <= row, new, -1e30)
    highest = jnp.maximum(
        jnp.max(old, axis=-1, keepdims=True), jnp.max(new, axis=-1, keepdims=True))
    old = jnp.exp2((old - highest) * factor)
    new = jnp.exp2((new - highest) * factor)
    denom = jnp.sum(old, axis=-1, keepdims=True) + jnp.sum(new, axis=-1, keepdims=True)
    mixed = jnp.dot(old.astype(jnp.bfloat16), vc_ref[...], preferred_element_type=jnp.float32)
    mixed += jnp.dot(new.astype(jnp.bfloat16), vn_ref[...], preferred_element_type=jnp.float32)
    out_ref[...] = (mixed / denom).astype(jnp.bfloat16)


def attend(qkv, keys, values, heads, key_heads):
    span = qkv.shape[0]
    past = keys.shape[0]
    share = heads // key_heads
    return pl.pallas_call(
        attend_kernel,
        out_shape=jax.ShapeDtypeStruct((span, heads * HEAD_DIM), jnp.bfloat16),
        grid=(heads,),
        in_specs=[
            pl.BlockSpec((span, HEAD_DIM), lambda h: (0, h)),
            pl.BlockSpec((span, HEAD_DIM), lambda h: (0, heads + h // share)),
            pl.BlockSpec((span, HEAD_DIM), lambda h: (0, heads + key_heads + h // share)),
            pl.BlockSpec((past, HEAD_DIM), lambda h: (0, h // share)),
            pl.BlockSpec((past, HEAD_DIM), lambda h: (0, h // share)),
        ],
        out_specs=pl.BlockSpec((span, HEAD_DIM), lambda h: (0, h)),
        compiler_params=pltpu.CompilerParams(vmem_limit_bytes=48 * 2**20),
    )(qkv, qkv, qkv, keys, values)


def rope_tables(span, offset):
    half = HEAD_DIM // 2
    inverse = np.float32(10000.0) ** (np.float32(-2.0) * np.arange(half, dtype=np.float32) / np.float32(HEAD_DIM))
    angles = (np.arange(span, dtype=np.float32) + np.float32(offset))[:, None] * inverse[None, :]
    angles = angles.astype(np.float64)
    cosine, sine = np.cos(angles), np.sin(angles)
    return (
        np.concatenate([cosine, cosine], axis=1).astype(np.float32),
        np.concatenate([-sine, sine], axis=1).astype(np.float32),
    )


def on_device(tokens, norm_gain, blocks, block_cols, key_cache, value_cache):
    tensor_count = lax.axis_size("tensor")
    count = lax.axis_size("fsdp")
    heads = Q_HEADS // tensor_count
    key_heads = KV_HEADS // tensor_count
    ncol = (heads + 2 * key_heads) * HEAD_DIM // BLK
    span = tokens.shape[1] * tensor_count
    slots = blocks.shape[1] // 2
    rows = max(D // BLK // count // 2, 1)
    named = block_cols[0].reshape(2, rows, slots // rows)
    match = named[..., None] == jnp.arange(ncol, dtype=jnp.int32)
    local = jnp.arange(slots, dtype=jnp.int32).reshape(1, rows, slots // rows, 1)
    places = slots + jnp.sum(jnp.where(match, local - slots, 0), axis=2)
    places = jnp.pad(places, ((0, 0), (0, -rows % 8), (0, -ncol % 128)))
    cosine, sine = rope_tables(span, key_cache.shape[1])
    qkv, _, _ = project(
        count, tokens[0], norm_gain, blocks[0].reshape(2, slots, BLK, BLK), places,
        jnp.asarray(cosine), jnp.asarray(sine), ncol, heads + key_heads)
    attended = attend(qkv, key_cache[0], value_cache[0], heads, key_heads)
    result = lax.all_to_all(attended, "tensor", split_axis=0, concat_axis=1, tiled=True)
    return result[None]


def solution(mesh):
    in_specs = (
        P(("groups", "fsdp"), "tensor", None),
        P(),
        P("tensor", "fsdp", None, None),
        P("tensor", "fsdp"),
        P(("groups", "fsdp"), None, "tensor"),
        P(("groups", "fsdp"), None, "tensor"),
    )
    out_specs = P(("groups", "fsdp"), "tensor", None)
    return jax.shard_map(
        on_device, mesh=mesh, in_specs=in_specs, out_specs=out_specs, check_vma=False
    )
```

```python
import functools
import math

import jax
import jax.numpy as jnp
import numpy as np
from jax import lax
from jax.experimental import pallas as pl
from jax.experimental.pallas import tpu as pltpu
from jax.sharding import PartitionSpec as P

D = 8192
Q_HEADS = 32
KV_HEADS = 4
HEAD_DIM = 128
BLK = 128
RCAP = 12
MESH = pl.DeviceIdType.MESH


def ring_shape(count):
    fast = 2 ** (int(math.log2(count)) // 2)
    return count // fast, fast


def ring_position(index, count):
    rows, fast = ring_shape(count)
    row, col = index // fast, index % fast
    turned = jnp.where(row % 2 == 0, col - 1, fast - 1 - col)
    inside = 1 + row * (fast - 1) + turned
    back = lax.rem(count - row, count)
    return jnp.where(col == 0, back, inside)


def ring_index(position, count):
    rows, fast = ring_shape(count)
    pos = jnp.where(position == 0, count, position)
    row_in = (pos - 1) // (fast - 1)
    k = (pos - 1) % (fast - 1)
    col_in = jnp.where(row_in % 2 == 0, 1 + k, fast - 1 - k)
    inside = row_in * fast + col_in
    back = (count - pos) * fast
    return jnp.where(pos <= rows * (fast - 1), inside, back)


def fused_kernel(count, ncol, rot_heads, tokens, gain, cos_ref, sin_ref, blocks, places,
                 qkv_out, weights, every_place,
                 mine, normed, stage_own, stage_sib, place_own, place_sib, panel, acc, ready,
                 ring_send, ring_recv, sib_send, sib_recv, own_send, own_recv,
                 tok_send, tok_recv, swap_send, swap_recv, local_sem, stage_sem):
    x = lax.axis_index("groups")
    f = lax.axis_index("fsdp")
    c = lax.axis_index("tensor")
    position = ring_position(f, count)
    step = 1 - 2 * c
    ahead = ring_index(lax.rem(position + step + count, count), count)
    behind = ring_index(lax.rem(position - step + count, count), count)
    slots = blocks.shape[1]
    sub = ring_send.shape[1] - 1
    piece = slots // sub
    half_rows = tokens.shape[0]
    width = tokens.shape[1]
    per_origin = width // count
    depth = panel.shape[0]
    owner = x == c
    guest = jnp.logical_not(owner)

    barrier = pltpu.get_barrier_semaphore()
    for peer in ((x, f, 1 - c), (1 - x, f, c), (1 - x, f, 1 - c), (x, ahead, c), (x, behind, c)):
        pl.semaphore_signal(barrier, inc=1, device_id=peer, device_id_type=MESH)
    pl.semaphore_wait(barrier, 5)

    def held(origin, half, k):
        if k == sub:
            return every_place.at[origin, half]
        return weights.at[origin, half, pl.ds(k * piece, piece)]

    def given(half, k):
        if k == sub:
            return places.at[half]
        return blocks.at[half, pl.ds(k * piece, piece)]

    def own(half, k):
        return pltpu.make_async_remote_copy(
            src_ref=given(half, k), dst_ref=held(f, half, k),
            send_sem=own_send.at[half, k], recv_sem=own_recv.at[half, k],
            device_id=(x, f, 1 - c), device_id_type=MESH)

    def from_behind(s):
        return ring_index(lax.rem(position - s * step + count * 2, count), count)

    def from_sibling(s):
        return ring_index(lax.rem(position + s * step + count * 2, count), count)

    def ring(s, k):
        ref = held(from_behind(s - 1), c, k)
        return pltpu.make_async_remote_copy(
            src_ref=ref, dst_ref=ref,
            send_sem=ring_send.at[s - 1, k], recv_sem=ring_recv.at[s - 1, k],
            device_id=(x, ahead, c), device_id_type=MESH)

    def ring_own(k):
        return pltpu.make_async_remote_copy(
            src_ref=given(c, k), dst_ref=held(f, c, k),
            send_sem=ring_send.at[0, k], recv_sem=ring_recv.at[0, k],
            device_id=(x, ahead, c), device_id_type=MESH)

    def arrived(s, k):
        ref = held(from_behind(s), c, k)
        return pltpu.make_async_remote_copy(
            src_ref=ref, dst_ref=ref,
            send_sem=ring_send.at[s - 1, k], recv_sem=ring_recv.at[s - 1, k],
            device_id=(x, ahead, c), device_id_type=MESH)

    def sibling(s, k):
        ref = held(from_behind(s), c, k)
        return pltpu.make_async_remote_copy(
            src_ref=ref, dst_ref=ref,
            send_sem=sib_send.at[s - 1, k], recv_sem=sib_recv.at[s - 1, k],
            device_id=(x, f, 1 - c), device_id_type=MESH)

    def sibling_arrived(s, k):
        ref = held(from_sibling(s), 1 - c, k)
        return pltpu.make_async_remote_copy(
            src_ref=ref, dst_ref=ref,
            send_sem=sib_send.at[s - 1, k], recv_sem=sib_recv.at[s - 1, k],
            device_id=(x, f, 1 - c), device_id_type=MESH)

    def token_rows(half):
        return normed.at[pl.ds(pl.multiple_of(half * half_rows, half_rows), half_rows)]

    def token(plane):
        return pltpu.make_async_remote_copy(
            src_ref=mine, dst_ref=token_rows(c),
            send_sem=tok_send.at[plane], recv_sem=tok_recv.at[c],
            device_id=(plane, f, x), device_id_type=MESH)

    def token_arrived(half):
        return pltpu.make_async_remote_copy(
            src_ref=mine, dst_ref=token_rows(half),
            send_sem=tok_send.at[0], recv_sem=tok_recv.at[half],
            device_id=(1 - x, f, x), device_id_type=MESH)

    def token_local():
        return pltpu.make_async_copy(mine, token_rows(c), local_sem.at[0])

    @pl.when(owner)
    def _():
        for k in range(sub + 1):
            own(1 - c, k).start()
        for k in (sub, 0, 1):
            ring_own(k).start()
        for k in range(sub + 1):
            own(c, k).start()

    @pl.when(guest)
    def _():
        for k in range(sub + 1):
            own(c, k).wait_recv()
        for k in (sub, 0, 1):
            ring(1, k).start()

    def norm_rows(i, carry):
        rows = pl.ds(pl.multiple_of(i * 16, 16), 16)
        wide = tokens[rows, :].astype(jnp.float32)
        variance = jnp.mean(wide * wide, axis=-1, keepdims=True)
        mine[rows, :] = (wide * lax.rsqrt(variance + 1e-05) * gain[...]).astype(jnp.bfloat16)
        return carry

    lax.fori_loop(0, half_rows // 16, norm_rows, 0)
    token(1 - x).start()

    @pl.when(owner)
    def _():
        token_local().start()

    @pl.when(guest)
    def _():
        token(x).start()

    for k in range(2, sub):
        ring(1, k - 2).wait_send()

        @pl.when(owner)
        def _():
            ring_own(k).start()

        @pl.when(guest)
        def _():
            ring(1, k).start()

    acc[...] = jnp.zeros_like(acc)
    for stage in (stage_own, stage_sib):
        stage[slots] = jnp.zeros((BLK, BLK), jnp.bfloat16)

    def pass_on(s, k):
        arrived(s, k).wait_recv()

        @pl.when(s < count - 1)
        def _():
            if k < sub:
                if k >= 2:
                    ring(s + 1, k - 2).wait_send()
                else:
                    ring(s, sub + k - 2).wait_send()
            ring(s + 1, k).start()

        sibling(s, k).start()

    order = [sub] + list(range(sub))

    def stage_copies(source, source_place, half, stage, place, which):
        return (
            pltpu.make_async_copy(source.at[half], stage.at[pl.ds(0, slots)], stage_sem.at[which, 0]),
            pltpu.make_async_copy(source_place.at[half], place, stage_sem.at[which, 1]),
        )

    def multiply(origin, half, stage, place):
        def fill(r, carry):
            rows = pl.ds(pl.multiple_of(r * BLK, BLK), BLK)
            for col in range(ncol):
                panel[rows, col * BLK:(col + 1) * BLK] = stage[place[r, col]]
            return carry

        lax.fori_loop(0, depth // BLK, fill, 0)
        start = origin * per_origin + half * (per_origin - depth)
        part = normed[:, pl.ds(pl.multiple_of(start, BLK), depth)]
        wide = 4 * BLK
        for j in range(0, ncol * BLK, wide):
            acc[:, j:j + wide] += jnp.dot(
                part, panel[:, j:j + wide], preferred_element_type=jnp.float32)

    def task(j, which):
        if which == 0:
            origin, half, stage, place = from_behind(j), c, stage_own, place_own
        else:
            origin, half, stage, place = from_sibling(j), 1 - c, stage_sib, place_sib

            @pl.when(j > 0)
            def _():
                for k in range(sub + 1):
                    sibling_arrived(j, k).wait_recv()
        copies = stage_copies(weights.at[origin], every_place.at[origin], half, stage, place, which)
        at_hand = jnp.logical_and(owner, j == 0)

        @pl.when(at_hand)
        def _():
            for copy in stage_copies(blocks, places, half, stage, place, which):
                copy.start()

        @pl.when(jnp.logical_not(at_hand))
        def _():
            for copy in copies:
                copy.start()

        for copy in copies:
            copy.wait()
        multiply(origin, half, stage, place)

    def early(s, carry):
        for k in order:
            pass_on(s, k)
        return carry

    lax.fori_loop(1, count // 2, early, 0)

    @pl.when(owner)
    def _():
        token_local().wait()
        token_arrived(1 - c).wait_recv()

    @pl.when(guest)
    def _():
        for k in range(sub + 1):
            own(1 - c, k).wait_recv()
        token_arrived(0).wait_recv()
        token_arrived(1).wait_recv()

    def late(s, carry):
        first = 2 * (s - count // 2)
        pass_on(s, sub)
        for k in range(sub):
            pass_on(s, k)
            for t in range(4):
                if min(t, sub - 1) != k:
                    continue
                if t < 2:
                    task(first, t)
                else:
                    @pl.when(first + 1 < count - 1)
                    def _():
                        task(first + 1, t - 2)
        return carry

    lax.fori_loop(count // 2, count, late, 0)
    task(count - 1, 0)
    task(count - 1, 1)

    part_width = 4 * BLK
    parts = ncol * BLK // part_width

    def swap(i):
        cols = pl.ds(i * part_width, part_width)
        return pltpu.make_async_remote_copy(
            src_ref=ready.at[:, cols], dst_ref=qkv_out.at[:, cols],
            send_sem=swap_send.at[i], recv_sem=swap_recv.at[i],
            device_id=(c, f, x), device_id_type=MESH)

    def keep(i):
        cols = pl.ds(i * part_width, part_width)
        return pltpu.make_async_copy(ready.at[:, cols], qkv_out.at[:, cols], swap_send.at[i])

    for i in range(parts):
        for h in range(i * part_width // BLK, (i + 1) * part_width // BLK):
            head = acc[:, h * BLK:(h + 1) * BLK]
            if h < rot_heads:
                head = head * cos_ref[...] + pltpu.roll(head, BLK // 2, 1) * sin_ref[...]
            ready[:, h * BLK:(h + 1) * BLK] = head.astype(jnp.bfloat16)

        @pl.when(owner)
        def _():
            keep(i).start()

        @pl.when(guest)
        def _():
            swap(i).start()

    ring(count - 1, sub - 2).wait_send()
    ring(count - 1, sub - 1).wait_send()

    def finish(s, carry):
        ring(s, sub).wait_send()
        for k in range(sub + 1):
            sibling(s, k).wait_send()
        return carry

    lax.fori_loop(1, count, finish, 0)
    token(1 - x).wait_send()

    @pl.when(owner)
    def _():
        for k in range(sub + 1):
            own(1 - c, k).wait_send()
            own(c, k).wait_send()
        for i in range(parts):
            keep(i).wait()

    @pl.when(guest)
    def _():
        token(x).wait_send()
        for i in range(parts):
            swap(i).wait_send()
            swap(i).wait_recv()


def project(count, tokens, norm_gain, blocks, places, cosine, sine, ncol, rot_heads):
    slots = blocks.shape[1]
    sub = max([option for option in (4, 3, 2) if slots % option == 0])
    half_rows, width = tokens.shape
    span = cosine.shape[0]
    depth = max(width // BLK // count // 2, 1) * BLK
    any_space = pl.BlockSpec(memory_space=pl.ANY)
    in_vmem = pl.BlockSpec(memory_space=pltpu.VMEM)
    dma = pltpu.SemaphoreType.DMA
    bf16 = jnp.bfloat16
    return pl.pallas_call(
        functools.partial(fused_kernel, count, ncol, rot_heads),
        out_shape=(
            jax.ShapeDtypeStruct((span, ncol * BLK), bf16),
            jax.ShapeDtypeStruct((count, 2, slots, BLK, BLK), bf16),
            jax.ShapeDtypeStruct((count,) + places.shape, jnp.int32),
        ),
        in_specs=[in_vmem] * 4 + [any_space] * 2,
        out_specs=(any_space,) * 3,
        scratch_shapes=[
            pltpu.VMEM((half_rows, width), bf16),
            pltpu.VMEM((span, width), bf16),
            pltpu.VMEM((slots + 1, BLK, BLK), bf16),
            pltpu.VMEM((slots + 1, BLK, BLK), bf16),
            pltpu.SMEM(places.shape[1:], jnp.int32),
            pltpu.SMEM(places.shape[1:], jnp.int32),
            pltpu.VMEM((depth, ncol * BLK), bf16),
            pltpu.VMEM((span, ncol * BLK), jnp.float32),
            pltpu.VMEM((span, ncol * BLK), bf16),
            dma((count - 1, sub + 1)), dma((count - 1, sub + 1)),
            dma((count - 1, sub + 1)), dma((count - 1, sub + 1)),
            dma((2, sub + 1)), dma((2, sub + 1)),
            dma((2,)), dma((2,)), dma((8,)), dma((8,)), dma((1,)), dma((2, 2)),
        ],
        compiler_params=pltpu.CompilerParams(
            collective_id=0, has_side_effects=True, vmem_limit_bytes=56 * 2**20),
    )(tokens, norm_gain[None], cosine, sine, blocks, places)


def attend_kernel(q_ref, kn_ref, vn_ref, kc_ref, vc_ref, out_ref):
    dims = (((1,), (1,)), ((), ()))
    factor = math.log2(math.e) / math.sqrt(HEAD_DIM)
    q = q_ref[...]
    old = lax.dot_general(q, kc_ref[...], dims, preferred_element_type=jnp.float32)
    new = lax.dot_general(q, kn_ref[...], dims, preferred_element_type=jnp.float32)
    row = lax.broadcasted_iota(jnp.int32, new.shape, 0)
    col = lax.broadcasted_iota(jnp.int32, new.shape, 1)
    new = jnp.where(col <= row, new, -1e30)
    highest = jnp.maximum(
        jnp.max(old, axis=-1, keepdims=True), jnp.max(new, axis=-1, keepdims=True))
    old = jnp.exp2((old - highest) * factor)
    new = jnp.exp2((new - highest) * factor)
    denom = jnp.sum(old, axis=-1, keepdims=True) + jnp.sum(new, axis=-1, keepdims=True)
    mixed = jnp.dot(old.astype(jnp.bfloat16), vc_ref[...], preferred_element_type=jnp.float32)
    mixed += jnp.dot(new.astype(jnp.bfloat16), vn_ref[...], preferred_element_type=jnp.float32)
    out_ref[...] = (mixed / denom).astype(jnp.bfloat16)


def attend(qkv, keys, values, heads, key_heads):
    span = qkv.shape[0]
    past = keys.shape[0]
    share = heads // key_heads
    return pl.pallas_call(
        attend_kernel,
        out_shape=jax.ShapeDtypeStruct((span, heads * HEAD_DIM), jnp.bfloat16),
        grid=(heads,),
        in_specs=[
            pl.BlockSpec((span, HEAD_DIM), lambda h: (0, h)),
            pl.BlockSpec((span, HEAD_DIM), lambda h: (0, heads + h // share)),
            pl.BlockSpec((span, HEAD_DIM), lambda h: (0, heads + key_heads + h // share)),
            pl.BlockSpec((past, HEAD_DIM), lambda h: (0, h // share)),
            pl.BlockSpec((past, HEAD_DIM), lambda h: (0, h // share)),
        ],
        out_specs=pl.BlockSpec((span, HEAD_DIM), lambda h: (0, h)),
        compiler_params=pltpu.CompilerParams(vmem_limit_bytes=48 * 2**20),
    )(qkv, qkv, qkv, keys, values)


def rope_tables(span, offset):
    half = HEAD_DIM // 2
    inverse = np.float32(10000.0) ** (np.float32(-2.0) * np.arange(half, dtype=np.float32) / np.float32(HEAD_DIM))
    angles = (np.arange(span, dtype=np.float32) + np.float32(offset))[:, None] * inverse[None, :]
    angles = angles.astype(np.float64)
    cosine, sine = np.cos(angles), np.sin(angles)
    return (
        np.concatenate([cosine, cosine], axis=1).astype(np.float32),
        np.concatenate([-sine, sine], axis=1).astype(np.float32),
    )


def on_device(tokens, norm_gain, blocks, block_cols, key_cache, value_cache):
    tensor_count = lax.axis_size("tensor")
    count = lax.axis_size("fsdp")
    heads = Q_HEADS // tensor_count
    key_heads = KV_HEADS // tensor_count
    ncol = (heads + 2 * key_heads) * HEAD_DIM // BLK
    span = tokens.shape[1] * tensor_count
    slots = blocks.shape[1] // 2
    rows = max(D // BLK // count // 2, 1)
    named = block_cols[0].reshape(2, rows, slots // rows)
    match = named[..., None] == jnp.arange(ncol, dtype=jnp.int32)
    local = jnp.arange(slots, dtype=jnp.int32).reshape(1, rows, slots // rows, 1)
    places = slots + jnp.sum(jnp.where(match, local - slots, 0), axis=2)
    places = jnp.pad(places, ((0, 0), (0, -rows % 8), (0, -ncol % 128)))
    cosine, sine = rope_tables(span, key_cache.shape[1])
    qkv, _, _ = project(
        count, tokens[0], norm_gain, blocks[0].reshape(2, slots, BLK, BLK), places,
        jnp.asarray(cosine), jnp.asarray(sine), ncol, heads + key_heads)
    attended = attend(qkv, key_cache[0], value_cache[0], heads, key_heads)
    result = lax.all_to_all(attended, "tensor", split_axis=0, concat_axis=1, tiled=True)
    return result[None]


def solution(mesh):
    in_specs = (
        P(("groups", "fsdp"), "tensor", None),
        P(),
        P("tensor", "fsdp", None, None),
        P("tensor", "fsdp"),
        P(("groups", "fsdp"), None, "tensor"),
        P(("groups", "fsdp"), None, "tensor"),
    )
    out_specs = P(("groups", "fsdp"), "tensor", None)
    return jax.shard_map(
        on_device, mesh=mesh, in_specs=in_specs, out_specs=out_specs, check_vma=False
    )
```

```python
import functools
import math

import jax
import jax.numpy as jnp
import numpy as np
from jax import lax
from jax.experimental import pallas as pl
from jax.experimental.pallas import tpu as pltpu
from jax.sharding import PartitionSpec as P

D = 8192
Q_HEADS = 32
KV_HEADS = 4
HEAD_DIM = 128
BLK = 128
RCAP = 12
MESH = pl.DeviceIdType.MESH


def ring_shape(count):
    fast = 2 ** (int(math.log2(count)) // 2)
    return count // fast, fast


def ring_position(index, count):
    rows, fast = ring_shape(count)
    row, col = index // fast, index % fast
    turned = jnp.where(row % 2 == 0, col - 1, fast - 1 - col)
    inside = 1 + row * (fast - 1) + turned
    back = lax.rem(count - row, count)
    return jnp.where(col == 0, back, inside)


def ring_index(position, count):
    rows, fast = ring_shape(count)
    pos = jnp.where(position == 0, count, position)
    row_in = (pos - 1) // (fast - 1)
    k = (pos - 1) % (fast - 1)
    col_in = jnp.where(row_in % 2 == 0, 1 + k, fast - 1 - k)
    inside = row_in * fast + col_in
    back = (count - pos) * fast
    return jnp.where(pos <= rows * (fast - 1), inside, back)


def fused_kernel(count, ncol, rot_heads, tokens, gain, cos_ref, sin_ref, blocks, places,
                 qkv_out, weights, every_place,
                 mine, normed, stage_own, stage_sib, place_own, place_sib, panel, acc, ready,
                 ring_send, ring_recv, sib_send, sib_recv, own_send, own_recv,
                 tok_send, tok_recv, swap_send, swap_recv, local_sem, stage_sem):
    x = lax.axis_index("groups")
    f = lax.axis_index("fsdp")
    c = lax.axis_index("tensor")
    position = ring_position(f, count)
    step = 1 - 2 * c
    ahead = ring_index(lax.rem(position + step + count, count), count)
    behind = ring_index(lax.rem(position - step + count, count), count)
    slots = blocks.shape[1]
    sub = ring_send.shape[1] - 1
    piece = slots // sub
    half_rows = tokens.shape[0]
    width = tokens.shape[1]
    per_origin = width // count
    depth = panel.shape[0]
    owner = x == c
    guest = jnp.logical_not(owner)

    barrier = pltpu.get_barrier_semaphore()
    for peer in ((x, f, 1 - c), (1 - x, f, c), (1 - x, f, 1 - c), (x, ahead, c), (x, behind, c)):
        pl.semaphore_signal(barrier, inc=1, device_id=peer, device_id_type=MESH)
    pl.semaphore_wait(barrier, 5)

    def held(origin, half, k):
        if k == sub:
            return every_place.at[origin, half]
        return weights.at[origin, half, pl.ds(k * piece, piece)]

    def given(half, k):
        if k == sub:
            return places.at[half]
        return blocks.at[half, pl.ds(k * piece, piece)]

    def own(half, k):
        return pltpu.make_async_remote_copy(
            src_ref=given(half, k), dst_ref=held(f, half, k),
            send_sem=own_send.at[half, k], recv_sem=own_recv.at[half, k],
            device_id=(x, f, 1 - c), device_id_type=MESH)

    def from_behind(s):
        return ring_index(lax.rem(position - s * step + count * 2, count), count)

    def from_sibling(s):
        return ring_index(lax.rem(position + s * step + count * 2, count), count)

    def ring(s, k):
        ref = held(from_behind(s - 1), c, k)
        return pltpu.make_async_remote_copy(
            src_ref=ref, dst_ref=ref,
            send_sem=ring_send.at[s - 1, k], recv_sem=ring_recv.at[s - 1, k],
            device_id=(x, ahead, c), device_id_type=MESH)

    def ring_own(k):
        return pltpu.make_async_remote_copy(
            src_ref=given(c, k), dst_ref=held(f, c, k),
            send_sem=ring_send.at[0, k], recv_sem=ring_recv.at[0, k],
            device_id=(x, ahead, c), device_id_type=MESH)

    def arrived(s, k):
        ref = held(from_behind(s), c, k)
        return pltpu.make_async_remote_copy(
            src_ref=ref, dst_ref=ref,
            send_sem=ring_send.at[s - 1, k], recv_sem=ring_recv.at[s - 1, k],
            device_id=(x, ahead, c), device_id_type=MESH)

    def sibling(s, k):
        ref = held(from_behind(s), c, k)
        return pltpu.make_async_remote_copy(
            src_ref=ref, dst_ref=ref,
            send_sem=sib_send.at[s - 1, k], recv_sem=sib_recv.at[s - 1, k],
            device_id=(x, f, 1 - c), device_id_type=MESH)

    def sibling_arrived(s, k):
        ref = held(from_sibling(s), 1 - c, k)
        return pltpu.make_async_remote_copy(
            src_ref=ref, dst_ref=ref,
            send_sem=sib_send.at[s - 1, k], recv_sem=sib_recv.at[s - 1, k],
            device_id=(x, f, 1 - c), device_id_type=MESH)

    def token_rows(half):
        return normed.at[pl.ds(pl.multiple_of(half * half_rows, half_rows), half_rows)]

    def token(plane):
        return pltpu.make_async_remote_copy(
            src_ref=mine, dst_ref=token_rows(c),
            send_sem=tok_send.at[plane], recv_sem=tok_recv.at[c],
            device_id=(plane, f, x), device_id_type=MESH)

    def token_arrived(half):
        return pltpu.make_async_remote_copy(
            src_ref=mine, dst_ref=token_rows(half),
            send_sem=tok_send.at[0], recv_sem=tok_recv.at[half],
            device_id=(1 - x, f, x), device_id_type=MESH)

    def token_local():
        return pltpu.make_async_copy(mine, token_rows(c), local_sem.at[0])

    @pl.when(owner)
    def _():
        for k in range(sub + 1):
            own(1 - c, k).start()
        for k in (sub, 0, 1):
            ring_own(k).start()
        for k in range(sub + 1):
            own(c, k).start()

    @pl.when(guest)
    def _():
        for k in range(sub + 1):
            own(c, k).wait_recv()
        for k in (sub, 0, 1):
            ring(1, k).start()

    def norm_rows(i, carry):
        rows = pl.ds(pl.multiple_of(i * 16, 16), 16)
        wide = tokens[rows, :].astype(jnp.float32)
        variance = jnp.mean(wide * wide, axis=-1, keepdims=True)
        mine[rows, :] = (wide * lax.rsqrt(variance + 1e-05) * gain[...]).astype(jnp.bfloat16)
        return carry

    lax.fori_loop(0, half_rows // 16, norm_rows, 0)
    token(1 - x).start()

    @pl.when(owner)
    def _():
        token_local().start()

    @pl.when(guest)
    def _():
        token(x).start()

    for k in range(2, sub):
        ring(1, k - 2).wait_send()

        @pl.when(owner)
        def _():
            ring_own(k).start()

        @pl.when(guest)
        def _():
            ring(1, k).start()

    acc[...] = jnp.zeros_like(acc)
    for stage in (stage_own, stage_sib):
        stage[slots] = jnp.zeros((BLK, BLK), jnp.bfloat16)

    def pass_on(s, k):
        arrived(s, k).wait_recv()

        @pl.when(s < count - 1)
        def _():
            if k < sub:
                if k >= 2:
                    ring(s + 1, k - 2).wait_send()
                else:
                    ring(s, sub + k - 2).wait_send()
            ring(s + 1, k).start()

        sibling(s, k).start()

    order = [sub] + list(range(sub))

    def stage_copies(source, source_place, half, stage, place, which):
        return (
            pltpu.make_async_copy(source.at[half], stage.at[pl.ds(0, slots)], stage_sem.at[which, 0]),
            pltpu.make_async_copy(source_place.at[half], place, stage_sem.at[which, 1]),
        )

    def multiply(origin, half, stage, place):
        def fill(r, carry):
            rows = pl.ds(pl.multiple_of(r * BLK, BLK), BLK)
            for col in range(ncol):
                panel[rows, col * BLK:(col + 1) * BLK] = stage[place[r, col]]
            return carry

        lax.fori_loop(0, depth // BLK, fill, 0)
        start = origin * per_origin + half * (per_origin - depth)
        part = normed[:, pl.ds(pl.multiple_of(start, BLK), depth)]
        wide = 4 * BLK
        for j in range(0, ncol * BLK, wide):
            acc[:, j:j + wide] += jnp.dot(
                part, panel[:, j:j + wide], preferred_element_type=jnp.float32)

    def task(j, which):
        if which == 0:
            origin, half, stage, place = from_behind(j), c, stage_own, place_own
        else:
            origin, half, stage, place = from_sibling(j), 1 - c, stage_sib, place_sib

            @pl.when(j > 0)
            def _():
                for k in range(sub + 1):
                    sibling_arrived(j, k).wait_recv()
        copies = stage_copies(weights.at[origin], every_place.at[origin], half, stage, place, which)
        at_hand = jnp.logical_and(owner, j == 0)

        @pl.when(at_hand)
        def _():
            for copy in stage_copies(blocks, places, half, stage, place, which):
                copy.start()

        @pl.when(jnp.logical_not(at_hand))
        def _():
            for copy in copies:
                copy.start()

        for copy in copies:
            copy.wait()
        multiply(origin, half, stage, place)

    def early(s, carry):
        for k in order:
            pass_on(s, k)
        return carry

    lax.fori_loop(1, count // 2, early, 0)

    @pl.when(owner)
    def _():
        token_local().wait()
        token_arrived(1 - c).wait_recv()

    @pl.when(guest)
    def _():
        for k in range(sub + 1):
            own(1 - c, k).wait_recv()
        token_arrived(0).wait_recv()
        token_arrived(1).wait_recv()

    def late(s, carry):
        first = 2 * (s - count // 2)
        pass_on(s, sub)
        for k in range(sub):
            pass_on(s, k)
            for t in range(4):
                if min(t, sub - 1) != k:
                    continue
                if t < 2:
                    task(first, t)
                else:
                    @pl.when(first + 1 < count - 1)
                    def _():
                        task(first + 1, t - 2)
        return carry

    lax.fori_loop(count // 2, count, late, 0)
    task(count - 1, 0)
    task(count - 1, 1)

    part_width = 4 * BLK
    parts = ncol * BLK // part_width

    def swap(i):
        cols = pl.ds(i * part_width, part_width)
        return pltpu.make_async_remote_copy(
            src_ref=ready.at[:, cols], dst_ref=qkv_out.at[:, cols],
            send_sem=swap_send.at[i], recv_sem=swap_recv.at[i],
            device_id=(c, f, x), device_id_type=MESH)

    def keep(i):
        cols = pl.ds(i * part_width, part_width)
        return pltpu.make_async_copy(ready.at[:, cols], qkv_out.at[:, cols], swap_send.at[i])

    for i in range(parts):
        for h in range(i * part_width // BLK, (i + 1) * part_width // BLK):
            head = acc[:, h * BLK:(h + 1) * BLK]
            if h < rot_heads:
                head = head * cos_ref[...] + pltpu.roll(head, BLK // 2, 1) * sin_ref[...]
            ready[:, h * BLK:(h + 1) * BLK] = head.astype(jnp.bfloat16)

        @pl.when(owner)
        def _():
            keep(i).start()

        @pl.when(guest)
        def _():
            swap(i).start()

    ring(count - 1, sub - 2).wait_send()
    ring(count - 1, sub - 1).wait_send()

    def finish(s, carry):
        ring(s, sub).wait_send()
        for k in range(sub + 1):
            sibling(s, k).wait_send()
        return carry

    lax.fori_loop(1, count, finish, 0)
    token(1 - x).wait_send()

    @pl.when(owner)
    def _():
        for k in range(sub + 1):
            own(1 - c, k).wait_send()
            own(c, k).wait_send()
        for i in range(parts):
            keep(i).wait()

    @pl.when(guest)
    def _():
        token(x).wait_send()
        for i in range(parts):
            swap(i).wait_send()
            swap(i).wait_recv()


def project(count, tokens, norm_gain, blocks, places, cosine, sine, ncol, rot_heads):
    slots = blocks.shape[1]
    sub = max([option for option in (4, 3, 2) if slots % option == 0])
    half_rows, width = tokens.shape
    span = cosine.shape[0]
    depth = max(width // BLK // count // 2, 1) * BLK
    any_space = pl.BlockSpec(memory_space=pl.ANY)
    in_vmem = pl.BlockSpec(memory_space=pltpu.VMEM)
    dma = pltpu.SemaphoreType.DMA
    bf16 = jnp.bfloat16
    return pl.pallas_call(
        functools.partial(fused_kernel, count, ncol, rot_heads),
        out_shape=(
            jax.ShapeDtypeStruct((span, ncol * BLK), bf16),
            jax.ShapeDtypeStruct((count, 2, slots, BLK, BLK), bf16),
            jax.ShapeDtypeStruct((count,) + places.shape, jnp.int32),
        ),
        in_specs=[in_vmem] * 4 + [any_space] * 2,
        out_specs=(any_space,) * 3,
        scratch_shapes=[
            pltpu.VMEM((half_rows, width), bf16),
            pltpu.VMEM((span, width), bf16),
            pltpu.VMEM((slots + 1, BLK, BLK), bf16),
            pltpu.VMEM((slots + 1, BLK, BLK), bf16),
            pltpu.SMEM(places.shape[1:], jnp.int32),
            pltpu.SMEM(places.shape[1:], jnp.int32),
            pltpu.VMEM((depth, ncol * BLK), bf16),
            pltpu.VMEM((span, ncol * BLK), jnp.float32),
            pltpu.VMEM((span, ncol * BLK), bf16),
            dma((count - 1, sub + 1)), dma((count - 1, sub + 1)),
            dma((count - 1, sub + 1)), dma((count - 1, sub + 1)),
            dma((2, sub + 1)), dma((2, sub + 1)),
            dma((2,)), dma((2,)), dma((8,)), dma((8,)), dma((1,)), dma((2, 2)),
        ],
        compiler_params=pltpu.CompilerParams(
            collective_id=0, has_side_effects=True, vmem_limit_bytes=56 * 2**20),
    )(tokens, norm_gain[None], cosine, sine, blocks, places)


def attend_kernel(q_ref, kn_ref, vn_ref, kc_ref, vc_ref, out_ref):
    dims = (((1,), (1,)), ((), ()))
    factor = math.log2(math.e) / math.sqrt(HEAD_DIM)
    for head in range(q_ref.shape[1] // HEAD_DIM):
        cols = slice(head * HEAD_DIM, (head + 1) * HEAD_DIM)
        q = q_ref[:, cols]
        old = lax.dot_general(q, kc_ref[...], dims, preferred_element_type=jnp.float32)
        new = lax.dot_general(q, kn_ref[...], dims, preferred_element_type=jnp.float32)
        row = lax.broadcasted_iota(jnp.int32, new.shape, 0)
        col = lax.broadcasted_iota(jnp.int32, new.shape, 1)
        new = jnp.where(col <= row, new, -1e30)
        highest = jnp.maximum(
            jnp.max(old, axis=-1, keepdims=True), jnp.max(new, axis=-1, keepdims=True))
        old = jnp.exp2((old - highest) * factor)
        new = jnp.exp2((new - highest) * factor)
        denom = jnp.sum(old, axis=-1, keepdims=True) + jnp.sum(new, axis=-1, keepdims=True)
        mixed = jnp.dot(old.astype(jnp.bfloat16), vc_ref[...], preferred_element_type=jnp.float32)
        mixed += jnp.dot(new.astype(jnp.bfloat16), vn_ref[...], preferred_element_type=jnp.float32)
        out_ref[:, cols] = (mixed / denom).astype(jnp.bfloat16)


def attend(qkv, keys, values, heads, key_heads):
    span = qkv.shape[0]
    past = keys.shape[0]
    pack = 4
    steps = heads // key_heads // pack
    return pl.pallas_call(
        attend_kernel,
        out_shape=jax.ShapeDtypeStruct((span, heads * HEAD_DIM), jnp.bfloat16),
        grid=(heads // pack,),
        in_specs=[
            pl.BlockSpec((span, pack * HEAD_DIM), lambda h: (0, h)),
            pl.BlockSpec((span, HEAD_DIM), lambda h: (0, heads + h // steps)),
            pl.BlockSpec((span, HEAD_DIM), lambda h: (0, heads + key_heads + h // steps)),
            pl.BlockSpec((past, HEAD_DIM), lambda h: (0, h // steps)),
            pl.BlockSpec((past, HEAD_DIM), lambda h: (0, h // steps)),
        ],
        out_specs=pl.BlockSpec((span, pack * HEAD_DIM), lambda h: (0, h)),
        compiler_params=pltpu.CompilerParams(vmem_limit_bytes=48 * 2**20),
    )(qkv, qkv, qkv, keys, values)


def rope_tables(span, offset):
    half = HEAD_DIM // 2
    inverse = np.float32(10000.0) ** (np.float32(-2.0) * np.arange(half, dtype=np.float32) / np.float32(HEAD_DIM))
    angles = (np.arange(span, dtype=np.float32) + np.float32(offset))[:, None] * inverse[None, :]
    angles = angles.astype(np.float64)
    cosine, sine = np.cos(angles), np.sin(angles)
    return (
        np.concatenate([cosine, cosine], axis=1).astype(np.float32),
        np.concatenate([-sine, sine], axis=1).astype(np.float32),
    )


def on_device(tokens, norm_gain, blocks, block_cols, key_cache, value_cache):
    tensor_count = lax.axis_size("tensor")
    count = lax.axis_size("fsdp")
    heads = Q_HEADS // tensor_count
    key_heads = KV_HEADS // tensor_count
    ncol = (heads + 2 * key_heads) * HEAD_DIM // BLK
    span = tokens.shape[1] * tensor_count
    slots = blocks.shape[1] // 2
    rows = max(D // BLK // count // 2, 1)
    named = block_cols[0].reshape(2, rows, slots // rows)
    match = named[..., None] == jnp.arange(ncol, dtype=jnp.int32)
    local = jnp.arange(slots, dtype=jnp.int32).reshape(1, rows, slots // rows, 1)
    places = slots + jnp.sum(jnp.where(match, local - slots, 0), axis=2)
    places = jnp.pad(places, ((0, 0), (0, -rows % 8), (0, -ncol % 128)))
    cosine, sine = rope_tables(span, key_cache.shape[1])
    qkv, _, _ = project(
        count, tokens[0], norm_gain, blocks[0].reshape(2, slots, BLK, BLK), places,
        jnp.asarray(cosine), jnp.asarray(sine), ncol, heads + key_heads)
    attended = attend(qkv, key_cache[0], value_cache[0], heads, key_heads)
    result = lax.all_to_all(attended, "tensor", split_axis=0, concat_axis=1, tiled=True)
    return result[None]


def solution(mesh):
    in_specs = (
        P(("groups", "fsdp"), "tensor", None),
        P(),
        P("tensor", "fsdp", None, None),
        P("tensor", "fsdp"),
        P(("groups", "fsdp"), None, "tensor"),
        P(("groups", "fsdp"), None, "tensor"),
    )
    out_specs = P(("groups", "fsdp"), "tensor", None)
    return jax.shard_map(
        on_device, mesh=mesh, in_specs=in_specs, out_specs=out_specs, check_vma=False
    )
```
